1024 devices in a mesh: row: 32 (over y, z_hi), col: 32 (over z_lo, x, core).
Axes of the slice: x: 8, y: 8, z: 8 (z_hi: 4, z_lo: 2; z = z_hi * 2 + z_lo), core: 2. Of those that a mesh axis runs over, the one named last changes fastest.
Arguments:
- tile_values: bfloat16 [32, 32, 96, 128, 128], P('row', 'col'), may hold values from -0.09375 to 0.09375
- tile_rows: int32 [32, 32, 96], P('row', 'col'), may hold values from 0 to 63
- tile_cols: int32 [32, 32, 96], P('row', 'col'), may hold values from 0 to 63
- tile_count: int32 [32, 32], P('row', 'col'), may hold values from 12 to 96, as said below
- vectors: bfloat16 [16, 262144], P(None, ('row', 'col')), may hold values from -6 to 6
Outputs:
- first_image: bfloat16 [16, 262144], P(None, ('row', 'col'))
- second_image: float32 [16, 262144], P(None, ('row', 'col'))
The draws below stay inside these ranges and needn't reach their ends.
Inputs may be any that keep to these rules, and one draw needn't show every extreme that they name: Each device's live slots are its first tile_count slots; the rest of its slots hold arbitrary data. Some device has all 96 slots live in every draw.
All inputs are finite; a program needn't handle non-finite values.
Results may differ from the reference program's by a relative error of at most 0.011.
Values may be sent and summed in bfloat16 or wider, within the bound.
No kernel may reach another device: no remote copies, remote signals or barrier semaphores. Data moves between devices by JAX's collectives and lax.ppermute only.
A program may use at most 32 MiB of HBM per device.

```python
import jax
import jax.numpy as jnp
from jax import lax

K = 16
TILE = 128
SLICET = 2
TILES_DEV = 96
ROWS = 262144
N_ROW = 32
N_COL = 32


def draw_tile_count(key, part):
    key = jax.random.fold_in(key, 5)
    key_base, key_heavy, key_place = jax.random.split(key, 3)
    lowest = max(1, TILES_DEV // 8)
    base = jax.random.randint(key_base, (N_ROW * N_COL,), lowest, max(lowest, TILES_DEV // 2) + 1)
    heavy = jax.random.randint(key_heavy, (N_ROW * N_COL,), 0, 16) == 0
    place = jax.random.randint(key_place, (), 0, N_ROW * N_COL)
    full = heavy | (jnp.arange(N_ROW * N_COL) == place)
    counts = jnp.where(full, TILES_DEV, base)
    return counts.reshape(N_ROW, N_COL).astype(jnp.int32)


def touch_ends(values, stream_key, least, top_value):
    spot = [jax.random.randint(jax.random.fold_in(stream_key, axis), (), 0, length) for axis, length in enumerate(values.shape)]
    longest = values.shape.index(max(values.shape))
    beside = spot[:longest] + [(spot[longest] + 1) % values.shape[longest]] + spot[longest + 1:]
    return values.at[tuple(spot)].set(least).at[tuple(beside)].set(top_value)


def block_scale(own_key, extent, cuts, least, largest):
    gain = 1.0
    for dim, parts in cuts:
        draws = jax.random.uniform(jax.random.fold_in(jax.random.fold_in(own_key, 6), dim), (parts,), jnp.float32, least / len(cuts), largest / len(cuts))
        gain = gain * jnp.repeat(jnp.exp(draws), extent[dim] // parts).reshape((-1,) + (1,) * (len(extent) - 1 - dim))
    return gain


def scatter_about(own_key, extent, deviation, bound, cuts=(), kind=jnp.bfloat16):
    values = jax.random.normal(own_key, extent, jnp.float32) * deviation
    if len(cuts) > 0:
        values = block_scale(own_key, extent, cuts, -0.22, 0.18) * values
    return jnp.clip(values, min=-bound, max=bound).astype(kind)


def setup_inputs(seed: int = 0) -> dict:
    keys = jax.random.split(jax.random.key(seed), 6)
    return {
        "tile_values": scatter_about(keys[0], (N_ROW, N_COL, TILES_DEV, TILE, TILE), (90 * TILES_DEV // SLICET) ** -0.5, 0.09375, ((0, 32), (1, 32))),
        "tile_rows": touch_ends(jax.random.randint(keys[1], (N_ROW, N_COL, TILES_DEV), 0, N_COL * SLICET), jax.random.fold_in(keys[1], 1), 0, (N_COL * SLICET) - 1).astype(jnp.int32),
        "tile_cols": touch_ends(jax.random.randint(keys[2], (N_ROW, N_COL, TILES_DEV), 0, N_ROW * SLICET), jax.random.fold_in(keys[2], 1), 0, (N_ROW * SLICET) - 1).astype(jnp.int32),
        "tile_count": draw_tile_count(jax.random.fold_in(keys[5], 71), 0),
        "vectors": scatter_about(keys[4], (K, ROWS), 1.0, 6.0, ((1, 1024),)),
    }


def contributions(tiles, row_index, col_index, live_count, row_vecs, col_vecs):
    is_live = jnp.arange(tiles.shape[0]) < live_count
    picked_cols = col_vecs[:, col_index]
    picked_rows = row_vecs[:, row_index]
    direct = jnp.einsum("nij,knj->kni", tiles, picked_cols)
    mirror = jnp.einsum("nij,kni->knj", tiles, picked_rows)
    row_marks = ((row_index[:, None] == jnp.arange(row_vecs.shape[1])[None, :]) & is_live[:, None]).astype(jnp.float32)
    col_marks = ((col_index[:, None] == jnp.arange(col_vecs.shape[1])[None, :]) & is_live[:, None]).astype(jnp.float32)
    return jnp.einsum("kni,ns->ksi", direct, row_marks), jnp.einsum("kni,ns->ksi", mirror, col_marks)


def hamiltonian(tile_values, tile_rows, tile_cols, tile_count, vectors):
    vec_count = vectors.shape[0]
    blocks = vectors.astype(jnp.float32).reshape(vec_count, N_ROW, N_COL, SLICET * TILE)

    def per_row(result, row_pos):
        row_vecs = blocks[:, row_pos].reshape(vec_count, N_COL * SLICET, TILE)

        def per_col(col_pos):
            col_vecs = blocks[:, :, col_pos].reshape(vec_count, N_ROW * SLICET, TILE)
            return contributions(tile_values[row_pos, col_pos].astype(jnp.float32), tile_rows[row_pos, col_pos],
                                 tile_cols[row_pos, col_pos], tile_count[row_pos, col_pos], row_vecs, col_vecs)

        direct_all, mirror_all = lax.map(per_col, jnp.arange(N_COL))
        direct_sum = jnp.sum(direct_all, axis=0).reshape(vec_count, N_COL, SLICET * TILE)
        result = result.at[:, row_pos].add(direct_sum)
        mirror_vals = mirror_all.reshape(N_COL, vec_count, N_ROW, SLICET * TILE).transpose(1, 2, 0, 3)
        return result + mirror_vals, None

    start_value = jnp.zeros((vec_count, N_ROW, N_COL, SLICET * TILE), jnp.float32)
    result, _ = lax.scan(per_row, start_value, jnp.arange(N_ROW))
    return result.reshape(vec_count, N_ROW * N_COL * SLICET * TILE)


def reference(tile_values, tile_rows, tile_cols, tile_count, vectors):
    first_image = hamiltonian(tile_values, tile_rows, tile_cols, tile_count, vectors).astype(jnp.bfloat16)
    second_image = hamiltonian(tile_values, tile_rows, tile_cols, tile_count, first_image)
    return first_image, second_image
```

```python
import jax
import jax.numpy as jnp
from jax import lax
from jax.experimental import pallas as pl
from jax.experimental.pallas import tpu as pltpu
from jax.sharding import PartitionSpec as P

UNROLL = 16
F32 = jnp.float32
BF16 = jnp.bfloat16


def products_kernel(rows_ref, cols_ref, count_ref, tiles_ref, row_seg_ref, col_seg_ref, direct_ref, mirror_ref, direct_acc, mirror_acc):
    slots = tiles_ref.shape[0]
    row_tiles = row_seg_ref.shape[0]
    col_tiles = col_seg_ref.shape[0]
    direct_acc[...] = jnp.zeros_like(direct_acc)
    mirror_acc[...] = jnp.zeros_like(mirror_acc)
    count = count_ref[0]

    def block(step, _):
        base = step * UNROLL
        results = []
        for u in range(UNROLL):
            n = base + u
            r, c = rows_ref[n], cols_ref[n]
            tile = tiles_ref[n]
            direct = lax.dot_general(col_seg_ref[c], tile, (((1,), (1,)), ((), ())), preferred_element_type=F32)
            mirror = lax.dot_general(row_seg_ref[r], tile, (((1,), (0,)), ((), ())), preferred_element_type=F32)
            live = n < count
            results.append((jnp.where(live, r, row_tiles), jnp.where(live, c, col_tiles), direct, mirror))
        for r, c, direct, mirror in results:
            direct_acc[r] += direct
            mirror_acc[c] += mirror
        return 0

    lax.fori_loop(0, slots // UNROLL, block, 0)
    direct_ref[...] = direct_acc[:row_tiles].astype(BF16)
    mirror_ref[...] = mirror_acc[:col_tiles].astype(BF16)


def products(rows, cols, count, tiles, row_seg, col_seg):
    vmem = pl.BlockSpec(memory_space=pltpu.VMEM)
    smem = pl.BlockSpec(memory_space=pltpu.SMEM)
    spare = lambda seg: pltpu.VMEM((seg.shape[0] + 1,) + seg.shape[1:], F32)
    return pl.pallas_call(
        products_kernel,
        out_shape=(jax.ShapeDtypeStruct(row_seg.shape, BF16), jax.ShapeDtypeStruct(col_seg.shape, BF16)),
        in_specs=[smem, smem, smem, vmem, vmem, vmem],
        out_specs=(vmem, vmem),
        scratch_shapes=[spare(row_seg), spare(col_seg)],
        compiler_params=pltpu.CompilerParams(vmem_limit_bytes=24 * 1024 * 1024),
        name="tile_products",
    )(rows, cols, count, tiles, row_seg, col_seg)


def sum_kernel(row_recv_ref, col_recv_ref, image_ref, *copies_ref):
    parts = row_recv_ref.shape[1]
    width = row_recv_ref.shape[-1]
    for h in range(parts):
        total = jnp.sum(row_recv_ref[:, h].astype(F32), axis=0) + jnp.sum(col_recv_ref[:, h].astype(F32), axis=0)
        value = total.astype(image_ref.dtype)
        image_ref[:, h * width:(h + 1) * width] = value
        if copies_ref:
            copies_ref[0][:, h] = jnp.broadcast_to(value[None], (copies_ref[0].shape[0],) + value.shape)


def sum_parts(row_recv, col_recv, dtype, copies):
    vmem = pl.BlockSpec(memory_space=pltpu.VMEM)
    parts, vec_count, width = row_recv.shape[1:]
    shapes = [jax.ShapeDtypeStruct((vec_count, parts * width), dtype)]
    if copies:
        shapes.append(jax.ShapeDtypeStruct(row_recv.shape, dtype))
    return pl.pallas_call(
        sum_kernel,
        out_shape=tuple(shapes),
        in_specs=[vmem, vmem],
        out_specs=(vmem,) * len(shapes),
        compiler_params=pltpu.CompilerParams(vmem_limit_bytes=16 * 1024 * 1024),
        name="sum_parts",
    )(row_recv, col_recv)


def exchange(parts, axis):
    return lax.all_to_all(parts, axis, 0, 0)


def per_device(tile_values, tile_rows, tile_cols, tile_count, vectors):
    tiles = tile_values[0, 0]
    rows, cols, count = tile_rows[0, 0], tile_cols[0, 0], tile_count[0]
    tile = tiles.shape[-1]
    vec_count, slice_len = vectors.shape
    parts = slice_len // tile
    peers = lax.axis_size("row")

    def image(copies, dtype, again):
        row_seg = exchange(copies, "col").reshape(-1, vec_count, tile)
        col_seg = exchange(copies, "row").reshape(-1, vec_count, tile)
        direct, mirror = products(rows, cols, count, tiles, row_seg, col_seg)
        row_recv = exchange(direct.reshape(copies.shape), "col")
        col_recv = exchange(mirror.reshape(copies.shape), "row")
        return sum_parts(row_recv, col_recv, dtype, again)

    own = vectors.reshape(vec_count, parts, tile).swapaxes(0, 1)
    copies = jnp.broadcast_to(own[None], (peers,) + own.shape)
    first_image, copies = image(copies, BF16, True)
    (second_image,) = image(copies, F32, False)
    return (first_image, second_image)


def solution(mesh):
    return jax.shard_map(
        per_device,
        mesh=mesh,
        in_specs=(
            P("row", "col", None, None, None),
            P("row", "col", None),
            P("row", "col", None),
            P("row", "col"),
            P(None, ("row", "col")),
        ),
        out_specs=(P(None, ("row", "col")), P(None, ("row", "col"))),
        check_vma=False,
    )
```

```python
import functools

import jax
import jax.numpy as jnp
from jax import lax
from jax.experimental import pallas as pl
from jax.experimental.pallas import tpu as pltpu
from jax.sharding import Mesh
from jax.sharding import PartitionSpec as P

UNROLL = 16
F32 = jnp.float32
BF16 = jnp.bfloat16
ROW = "row"
NEAR = "near"
CORE = "core"
CORES = 2
VMEM = pl.BlockSpec(memory_space=pltpu.VMEM)
SMEM = pl.BlockSpec(memory_space=pltpu.SMEM)


def by_core(tile_row, parts, near):
    part, owner = tile_row % parts, tile_row // parts
    return owner // CORES * parts + part, owner % CORES, near * parts


def mirror_kernel(parts, near, rows_ref, cols_ref, count_ref, tiles_ref, row_seg_ref, out_ref, acc):
    slots, col_tiles = tiles_ref.shape[0], out_ref.shape[0]
    acc[...] = jnp.zeros_like(acc)
    count = count_ref[0]

    def block(step, _):
        results = []
        for u in range(UNROLL):
            n = step * UNROLL + u
            place, core, half = by_core(rows_ref[n], parts, near)
            picked = row_seg_ref[core * half + place]
            product = lax.dot_general(picked, tiles_ref[n], (((1,), (0,)), ((), ())), preferred_element_type=F32)
            results.append((jnp.where(n < count, cols_ref[n], col_tiles), product))
        for c, product in results:
            acc[c] += product
        return 0

    lax.fori_loop(0, slots // UNROLL, block, 0)
    out_ref[...] = acc[:col_tiles].astype(BF16)


def direct_kernel(parts, near, rows_ref, cols_ref, count_ref, core_ref, tiles_ref, col_seg_ref, keep_ref, send_ref, acc):
    slots, half = tiles_ref.shape[0], keep_ref.shape[0]
    acc[...] = jnp.zeros_like(acc)
    count, mine = count_ref[0], core_ref[0]

    def block(step, _):
        results = []
        for u in range(UNROLL):
            n = step * UNROLL + u
            picked = col_seg_ref[cols_ref[n]]
            product = lax.dot_general(picked, tiles_ref[n], (((1,), (1,)), ((), ())), preferred_element_type=F32)
            place, core, _ = by_core(rows_ref[n], parts, near)
            where = jnp.where(core == mine, 0, half) + place
            results.append((jnp.where(n < count, where, 2 * half), product))
        for r, product in results:
            acc[r] += product
        return 0

    lax.fori_loop(0, slots // UNROLL, block, 0)
    keep_ref[...] = acc[:half]
    send_ref[...] = acc[half:2 * half].astype(BF16)


def half_kernel(keep_ref, recv_ref, out_ref):
    out_ref[...] = (keep_ref[...] + recv_ref[...].astype(F32)).astype(BF16)


def sum_kernel(row_recv_ref, near_recv_ref, image_ref, *copies_ref):
    parts, width = row_recv_ref.shape[1], row_recv_ref.shape[-1]
    for h in range(parts):
        total = jnp.sum(row_recv_ref[:, h].astype(F32), axis=0) + jnp.sum(near_recv_ref[:, h].astype(F32), axis=0)
        value = total.astype(image_ref.dtype)
        image_ref[:, h * width:(h + 1) * width] = value
        for ref in copies_ref:
            ref[:, h] = jnp.broadcast_to(value[None], (ref.shape[0],) + value.shape)


def call(kernel, name, in_specs, shapes, scratch, flops, moved, *args):
    return pl.pallas_call(
        kernel,
        out_shape=tuple(jax.ShapeDtypeStruct(s, d) for s, d in shapes),
        in_specs=in_specs,
        out_specs=(VMEM,) * len(shapes),
        scratch_shapes=scratch,
        compiler_params=pltpu.CompilerParams(vmem_limit_bytes=20 * 1024 * 1024),
        cost_estimate=pl.CostEstimate(flops=flops, bytes_accessed=moved, transcendentals=0),
        name=name,
    )(*args)


def per_device(tile_values, tile_rows, tile_cols, tile_count, vectors):
    tiles = tile_values[0, 0]
    rows, cols, count = tile_rows[0, 0], tile_cols[0, 0], tile_count[0]
    slots, tile = tiles.shape[0], tiles.shape[-1]
    vec_count, slice_len = vectors.shape
    parts = slice_len // tile
    peers, near = lax.axis_size(ROW), lax.axis_size(NEAR)
    own_core = lax.axis_index(CORE).astype(jnp.int32).reshape(1)
    piece = (parts, vec_count, tile)
    half = (near * parts, vec_count, tile)
    seg = (peers * parts, vec_count, tile)
    flops, moved = 2 * slots * vec_count * tile * tile, 2 * tiles.size
    acc = lambda n: [pltpu.VMEM((n + 1, vec_count, tile), F32)]

    def image(near_copies, row_copies, dtype, again):
        near_recv = lax.all_to_all(near_copies, NEAR, 0, 0)
        col_seg = lax.all_to_all(row_copies, ROW, 0, 0).reshape(seg)
        row_seg = lax.all_gather(near_recv.reshape(half), CORE, axis=0, tiled=True)
        (mirror,) = call(
            functools.partial(mirror_kernel, parts, near), "mirror_products", [SMEM] * 3 + [VMEM] * 2,
            [(seg, BF16)], acc(seg[0]), flops, moved, rows, cols, count, tiles, row_seg)
        row_recv = lax.all_to_all(mirror.reshape((peers,) + piece), ROW, 0, 0)
        keep, send = call(
            functools.partial(direct_kernel, parts, near), "direct_products", [SMEM] * 4 + [VMEM] * 2,
            [(half, F32), (half, BF16)], acc(CORES * half[0]), flops, moved, rows, cols, count, own_core, tiles, col_seg)
        recv = lax.ppermute(send, CORE, [(0, 1), (1, 0)])
        (chip,) = call(half_kernel, "chip_sum", [VMEM] * 2, [(half, BF16)], [], keep.size, 8 * keep.size, keep, recv)
        near_recv = lax.all_to_all(chip.reshape((near,) + piece), NEAR, 0, 0)
        shapes = [((vec_count, slice_len), dtype)]
        if again:
            shapes += [((near,) + piece, dtype), ((peers,) + piece, dtype)]
        return call(sum_kernel, "sum_parts", [VMEM] * 2, shapes, [], 2 * row_recv.size, 4 * row_recv.size, row_recv, near_recv)

    own = vectors.reshape(vec_count, parts, tile).swapaxes(0, 1)
    spread = lambda n: jnp.broadcast_to(own[None], (n,) + own.shape)
    first_image, near_copies, row_copies = image(spread(near), spread(peers), BF16, True)
    (second_image,) = image(near_copies, row_copies, F32, False)
    return (first_image, second_image)


def solution(mesh):
    rows, cols = mesh.devices.shape
    split = Mesh(mesh.devices.reshape(rows, cols // CORES, CORES), (ROW, NEAR, CORE))
    both = (NEAR, CORE)
    whole = (ROW, NEAR, CORE)
    return jax.shard_map(
        per_device,
        mesh=split,
        in_specs=(P(ROW, both, None, None, None), P(ROW, both, None), P(ROW, both, None), P(ROW, both), P(None, whole)),
        out_specs=(P(None, whole), P(None, whole)),
        check_vma=False,
    )
```

```python
import functools

import jax
import jax.numpy as jnp
from jax import lax
from jax.experimental import pallas as pl
from jax.experimental.pallas import tpu as pltpu
from jax.sharding import Mesh
from jax.sharding import PartitionSpec as P

UNROLL = 16
F32 = jnp.float32
BF16 = jnp.bfloat16
ROW = "row"
ZLO = "z_lo"
LINE = "x"
CORE = "core"
ZLOS, LINES, CORES = 2, 8, 2
QUADS = ZLOS * CORES
VMEM = pl.BlockSpec(memory_space=pltpu.VMEM)
SMEM = pl.BlockSpec(memory_space=pltpu.SMEM)


def position(tile_row, parts):
    part, owner = tile_row & (parts - 1), tile_row >> (parts.bit_length() - 1)
    core, line = owner & (CORES - 1), (owner >> 1) & (LINES - 1)
    return owner >> (CORES * LINES).bit_length() - 1, core, line * parts + part


def mirror_kernel(parts, rows_ref, cols_ref, count_ref, tiles_ref, row_seg_ref, out_ref, acc):
    slots, col_tiles = tiles_ref.shape[0], out_ref.shape[0]
    quad = row_seg_ref.shape[0] // QUADS
    acc[...] = jnp.zeros_like(acc)
    count = count_ref[0]

    def block(step, _):
        results = []
        for u in range(UNROLL):
            n = step * UNROLL + u
            z_lo, core, place = position(rows_ref[n], parts)
            picked = row_seg_ref[(core * ZLOS + z_lo) * quad + place]
            product = lax.dot_general(picked, tiles_ref[n], (((1,), (0,)), ((), ())), preferred_element_type=F32)
            results.append((jnp.where(n < count, cols_ref[n], col_tiles), product))
        for c, product in results:
            acc[c] += product
        return 0

    lax.fori_loop(0, slots // UNROLL, block, 0)
    out_ref[...] = acc[:col_tiles].astype(BF16)


def direct_kernel(parts, rows_ref, cols_ref, count_ref, place_ref, tiles_ref, col_seg_ref, keep_ref, core_ref, z_lo_ref, both_ref, acc):
    slots, quad = tiles_ref.shape[0], keep_ref.shape[0]
    acc[...] = jnp.zeros_like(acc)
    count, my_z_lo, my_core = count_ref[0], place_ref[0], place_ref[1]

    def block(step, _):
        results = []
        for u in range(UNROLL):
            n = step * UNROLL + u
            picked = col_seg_ref[cols_ref[n]]
            product = lax.dot_general(picked, tiles_ref[n], (((1,), (1,)), ((), ())), preferred_element_type=F32)
            z_lo, core, place = position(rows_ref[n], parts)
            where = ((z_lo ^ my_z_lo) * CORES + (core ^ my_core)) * quad + place
            results.append((jnp.where(n < count, where, QUADS * quad), product))
        for r, product in results:
            acc[r] += product
        return 0

    lax.fori_loop(0, slots // UNROLL, block, 0)
    keep_ref[...] = acc[:quad]
    for q, ref in enumerate((core_ref, z_lo_ref, both_ref), 1):
        ref[...] = acc[q * quad:(q + 1) * quad].astype(BF16)


def quad_kernel(keep_ref, core_ref, z_lo_ref, both_ref, out_ref):
    out_ref[...] = (keep_ref[...] + core_ref[...].astype(F32) + (z_lo_ref[...].astype(F32) + both_ref[...].astype(F32))).astype(BF16)


def row_sum_kernel(recv_ref, out_ref):
    for h in range(recv_ref.shape[1]):
        out_ref[h] = jnp.sum(recv_ref[:, h].astype(F32), axis=0)


def image_kernel(row_sum_ref, line_recv_ref, image_ref, *copies_ref):
    parts, width = row_sum_ref.shape[0], row_sum_ref.shape[-1]
    for h in range(parts):
        value = (row_sum_ref[h] + jnp.sum(line_recv_ref[:, h].astype(F32), axis=0)).astype(image_ref.dtype)
        image_ref[:, h * width:(h + 1) * width] = value
        for ref in copies_ref:
            ref[:, h] = jnp.broadcast_to(value[None], (ref.shape[0],) + value.shape)


def call(kernel, name, in_specs, shapes, scratch, flops, moved, *args):
    return pl.pallas_call(
        kernel,
        out_shape=tuple(jax.ShapeDtypeStruct(s, d) for s, d in shapes),
        in_specs=in_specs,
        out_specs=(VMEM,) * len(shapes),
        scratch_shapes=scratch,
        compiler_params=pltpu.CompilerParams(vmem_limit_bytes=12 * 1024 * 1024),
        cost_estimate=pl.CostEstimate(flops=flops, bytes_accessed=moved, transcendentals=0),
        name=name,
    )(*args)


def per_device(tile_values, tile_rows, tile_cols, tile_count, vectors):
    tiles = tile_values[0, 0]
    rows, cols, count = tile_rows[0, 0], tile_cols[0, 0], tile_count[0]
    slots, tile = tiles.shape[0], tiles.shape[-1]
    vec_count, slice_len = vectors.shape
    parts = slice_len // tile
    peers = lax.axis_size(ROW)
    place = jnp.stack([lax.axis_index(ZLO), lax.axis_index(CORE)]).astype(jnp.int32)
    piece = (parts, vec_count, tile)
    quad = (LINES * parts, vec_count, tile)
    seg = (peers * parts, vec_count, tile)
    flops, moved = 2 * slots * vec_count * tile * tile, 2 * tiles.size
    acc = lambda n: [pltpu.VMEM((n + 1, vec_count, tile), F32)]

    def image(line_copies, row_copies, dtype, again):
        line_recv = lax.all_to_all(line_copies, LINE, 0, 0)
        col_seg = lax.all_to_all(row_copies, ROW, 0, 0).reshape(seg)
        two_lines = lax.all_gather(line_recv.reshape(quad), ZLO, axis=0, tiled=True)
        row_seg = lax.all_gather(two_lines, CORE, axis=0, tiled=True)
        (mirror,) = call(
            functools.partial(mirror_kernel, parts), "mirror_products", [SMEM] * 3 + [VMEM] * 2,
            [(seg, BF16)], acc(seg[0]), flops, moved, rows, cols, count, tiles, row_seg)
        row_recv = lax.all_to_all(mirror.reshape((peers,) + piece), ROW, 0, 0)
        keep, to_core, to_z_lo, to_both = call(
            functools.partial(direct_kernel, parts), "direct_products", [SMEM] * 4 + [VMEM] * 2,
            [(quad, F32)] + [(quad, BF16)] * 3, acc(QUADS * quad[0]), flops, moved, rows, cols, count, place, tiles, col_seg)
        recv = [
            lax.ppermute(to_both, (ZLO, CORE), [(i, QUADS - 1 - i) for i in range(QUADS)]),
            lax.ppermute(to_z_lo, ZLO, [(0, 1), (1, 0)]),
            lax.ppermute(to_core, CORE, [(0, 1), (1, 0)]),
        ]
        (line,) = call(quad_kernel, "quad_sum", [VMEM] * 4, [(quad, BF16)], [], 4 * keep.size, 12 * keep.size, keep, *recv)
        line_recv = lax.all_to_all(line.reshape((LINES,) + piece), LINE, 0, 0)
        (row_sum,) = call(row_sum_kernel, "row_sum", [VMEM], [(piece, F32)], [], row_recv.size, 2 * row_recv.size, row_recv)
        shapes = [((vec_count, slice_len), dtype)]
        if again:
            shapes += [((LINES,) + piece, dtype), ((peers,) + piece, dtype)]
        return call(image_kernel, "image", [VMEM] * 2, shapes, [], line_recv.size, 4 * line_recv.size, row_sum, line_recv)

    own = vectors.reshape(vec_count, parts, tile).swapaxes(0, 1)
    spread = lambda n: jnp.broadcast_to(own[None], (n,) + own.shape)
    first_image, line_copies, row_copies = image(spread(LINES), spread(peers), BF16, True)
    (second_image,) = image(line_copies, row_copies, F32, False)
    return (first_image, second_image)


def solution(mesh):
    rows = mesh.devices.shape[0]
    split = Mesh(mesh.devices.reshape(rows, ZLOS, LINES, CORES), (ROW, ZLO, LINE, CORE))
    col = (ZLO, LINE, CORE)
    whole = (ROW,) + col
    return jax.shard_map(
        per_device,
        mesh=split,
        in_specs=(P(ROW, col, None, None, None), P(ROW, col, None), P(ROW, col, None), P(ROW, col), P(None, whole)),
        out_specs=(P(None, whole), P(None, whole)),
        check_vma=False,
    )
```

```python
import functools

import jax
import jax.numpy as jnp
from jax import lax
from jax.experimental import pallas as pl
from jax.experimental.pallas import tpu as pltpu
from jax.sharding import Mesh
from jax.sharding import PartitionSpec as P

UNROLL = 16
F32 = jnp.float32
BF16 = jnp.bfloat16
Y, ZHI, NEAR, CORE = "y", "z_hi", "near", "core"
ROW = (Y, ZHI)
ZHIS, CORES = 4, 2
VMEM = pl.BlockSpec(memory_space=pltpu.VMEM)
SMEM = pl.BlockSpec(memory_space=pltpu.SMEM)


def by_core(tile_row, parts):
    part, owner = tile_row & (parts - 1), tile_row >> (parts.bit_length() - 1)
    return owner & (CORES - 1), (owner >> (CORES.bit_length() - 1)) * parts + part


def mirror_kernel(parts, rows_ref, cols_ref, count_ref, tiles_ref, row_seg_ref, out_ref, acc):
    slots, col_tiles = tiles_ref.shape[0], out_ref.shape[0]
    half = row_seg_ref.shape[0] // CORES
    acc[...] = jnp.zeros_like(acc)
    count = count_ref[0]

    def block(step, _):
        results = []
        for u in range(UNROLL):
            n = step * UNROLL + u
            core, place = by_core(rows_ref[n], parts)
            product = lax.dot_general(row_seg_ref[core * half + place], tiles_ref[n], (((1,), (0,)), ((), ())), preferred_element_type=F32)
            results.append((jnp.where(n < count, cols_ref[n], col_tiles), product))
        for c, product in results:
            acc[c] += product
        return 0

    lax.fori_loop(0, slots // UNROLL, block, 0)
    out_ref[...] = acc[:col_tiles].astype(BF16)


def direct_kernel(parts, rows_ref, cols_ref, count_ref, at_ref, tiles_ref, col_seg_ref, keep_ref, send_ref, acc):
    slots, half = tiles_ref.shape[0], keep_ref.shape[0]
    acc[...] = jnp.zeros_like(acc)
    count, mine = count_ref[0], at_ref[0]

    def block(step, _):
        results = []
        for u in range(UNROLL):
            n = step * UNROLL + u
            product = lax.dot_general(col_seg_ref[cols_ref[n]], tiles_ref[n], (((1,), (1,)), ((), ())), preferred_element_type=F32)
            core, place = by_core(rows_ref[n], parts)
            results.append((jnp.where(n < count, (core ^ mine) * half + place, CORES * half), product))
        for r, product in results:
            acc[r] += product
        return 0

    lax.fori_loop(0, slots // UNROLL, block, 0)
    keep_ref[...] = acc[:half]
    send_ref[...] = acc[half:2 * half].astype(BF16)


def half_kernel(keep_ref, recv_ref, out_ref):
    out_ref[...] = (keep_ref[...] + recv_ref[...].astype(F32)).astype(BF16)


def total(ref, *index):
    return jnp.sum(ref[(slice(None),) + index].astype(F32), axis=0)


def write_image(image_ref, part, value):
    width = value.shape[-1]
    image_ref[:, part * width:(part + 1) * width] = value


def partial_kernel(at_ref, y_recv_ref, near_recv_ref, out_ref, acc):
    z_his, parts = y_recv_ref.shape[1:3]
    for z in range(z_his):
        for h in range(parts):
            acc[z, h] = total(y_recv_ref, z, h)
    for h in range(parts):
        acc[at_ref[1], h] += total(near_recv_ref, h)
    out_ref[...] = jnp.broadcast_to(acc[...].astype(BF16)[None], out_ref.shape)


def middle_kernel(at_ref, z_recv_ref, image_ref, near_ref, y_ref, acc):
    z_his, parts = z_recv_ref.shape[1:3]
    for z in range(z_his):
        for h in range(parts):
            value = total(z_recv_ref, z, h).astype(BF16)
            acc[z, h] = value
            y_ref[:, z, h] = jnp.broadcast_to(value[None], (y_ref.shape[0],) + value.shape)
    for h in range(parts):
        value = acc[at_ref[1], h]
        write_image(image_ref, h, value)
        near_ref[:, h] = jnp.broadcast_to(value[None], (near_ref.shape[0],) + value.shape)


def last_kernel(row_recv_ref, near_recv_ref, image_ref):
    for h in range(row_recv_ref.shape[1]):
        write_image(image_ref, h, total(row_recv_ref, h) + total(near_recv_ref, h))


def call(kernel, name, in_specs, shapes, scratch, flops, moved, *args):
    return pl.pallas_call(
        kernel,
        out_shape=tuple(jax.ShapeDtypeStruct(s, d) for s, d in shapes),
        in_specs=in_specs,
        out_specs=(VMEM,) * len(shapes),
        scratch_shapes=scratch,
        compiler_params=pltpu.CompilerParams(vmem_limit_bytes=12 * 1024 * 1024),
        cost_estimate=pl.CostEstimate(flops=flops, bytes_accessed=moved, transcendentals=0),
        name=name,
    )(*args)


def per_device(tile_values, tile_rows, tile_cols, tile_count, vectors):
    tiles = tile_values[0, 0]
    rows, cols, count = tile_rows[0, 0], tile_cols[0, 0], tile_count[0]
    slots, tile = tiles.shape[0], tiles.shape[-1]
    vec_count, slice_len = vectors.shape
    parts = slice_len // tile
    ys, z_his, near = lax.axis_size(Y), lax.axis_size(ZHI), lax.axis_size(NEAR)
    at = jnp.stack([lax.axis_index(CORE), lax.axis_index(ZHI)]).astype(jnp.int32)
    piece = (parts, vec_count, tile)
    half = (near * parts, vec_count, tile)
    seg = (ys * z_his * parts, vec_count, tile)
    flops, moved = 2 * slots * vec_count * tile * tile, 2 * tiles.size
    acc = lambda n: [pltpu.VMEM((n + 1, vec_count, tile), F32)]

    def application(near_copies, row_copies, gather_axis, sum_axis, sum_shape):
        near_recv = lax.all_to_all(near_copies, NEAR, 0, 0)
        col_seg = lax.all_to_all(row_copies, gather_axis, 0, 0).reshape(seg)
        row_seg = lax.all_gather(near_recv.reshape(half), CORE, axis=0, tiled=True)
        (mirror,) = call(
            functools.partial(mirror_kernel, parts), "mirror_products", [SMEM] * 3 + [VMEM] * 2,
            [(seg, BF16)], acc(seg[0]), flops, moved, rows, cols, count, tiles, row_seg)
        row_recv = lax.all_to_all(mirror.reshape(sum_shape + piece), sum_axis, 0, 0)
        keep, send = call(
            functools.partial(direct_kernel, parts), "direct_products", [SMEM] * 4 + [VMEM] * 2,
            [(half, F32), (half, BF16)], acc(CORES * half[0]), flops, moved, rows, cols, count, at, tiles, col_seg)
        recv = lax.ppermute(send, CORE, [(0, 1), (1, 0)])
        (chip,) = call(half_kernel, "chip_sum", [VMEM] * 2, [(half, BF16)], [], keep.size, 8 * keep.size, keep, recv)
        return row_recv, lax.all_to_all(chip.reshape((near,) + piece), NEAR, 0, 0)

    own = vectors.reshape(vec_count, parts, tile).swapaxes(0, 1)
    spread = lambda n: jnp.broadcast_to(own[None], (n,) + own.shape)
    plane = (z_his,) + piece
    y_recv, near_recv = application(spread(near), spread(ys * z_his), ROW, Y, (ys, z_his))
    (partials,) = call(
        partial_kernel, "partial_sums", [SMEM] + [VMEM] * 2, [((z_his,) + plane, BF16)], [pltpu.VMEM(plane, F32)],
        2 * y_recv.size, 4 * y_recv.size, at, y_recv, near_recv)
    z_recv = lax.all_to_all(partials, ZHI, 0, 0)
    first_image, near_copies, y_copies = call(
        middle_kernel, "middle_image", [SMEM, VMEM],
        [(vectors.shape, BF16), ((near,) + piece, BF16), ((ys,) + plane, BF16)], [pltpu.VMEM(plane, BF16)],
        2 * y_recv.size, 4 * y_recv.size, at, z_recv)
    row_recv, near_recv = application(near_copies, y_copies, Y, ROW, (ys * z_his,))
    (second_image,) = call(
        last_kernel, "last_image", [VMEM] * 2, [(vectors.shape, F32)], [], 2 * row_recv.size, 4 * row_recv.size, row_recv, near_recv)
    return (first_image, second_image)


def solution(mesh):
    rows, cols = mesh.devices.shape
    split = Mesh(mesh.devices.reshape(rows // ZHIS, ZHIS, cols // CORES, CORES), ROW + (NEAR, CORE))
    col = (NEAR, CORE)
    whole = ROW + col
    return jax.shard_map(
        per_device,
        mesh=split,
        in_specs=(P(ROW, col, None, None, None), P(ROW, col, None), P(ROW, col, None), P(ROW, col), P(None, whole)),
        out_specs=(P(None, whole), P(None, whole)),
        check_vma=False,
    )
```

```python
import jax
import jax.numpy as jnp
from jax import lax
from jax.experimental import pallas as pl
from jax.experimental.pallas import tpu as pltpu
from jax.sharding import Mesh
from jax.sharding import PartitionSpec as P

UNROLL = 16
F32 = jnp.float32
BF16 = jnp.bfloat16
ROW, NEAR, CORE = "row", "near", "core"
CORES = 2
VMEM = pl.BlockSpec(memory_space=pltpu.VMEM)
SMEM = pl.BlockSpec(memory_space=pltpu.SMEM)


def by_core(tile_row, parts):
    part, owner = tile_row & (parts - 1), tile_row >> (parts.bit_length() - 1)
    return owner & (CORES - 1), (owner >> (CORES.bit_length() - 1)) * parts + part


def start_kernel(vectors_ref, count_ref, own_ref, copies_ref, counts_ref):
    width = own_ref.shape[-1]
    for h in range(own_ref.shape[0]):
        value = vectors_ref[:, h * width:(h + 1) * width]
        own_ref[h] = value
        copies_ref[:, h] = jnp.broadcast_to(value[None], (copies_ref.shape[0],) + value.shape)
    counts_ref[...] = jnp.broadcast_to(count_ref[...], counts_ref.shape)


def mirror_kernel(rows_ref, cols_ref, count_ref, tiles_ref, row_seg_ref, own_ref, packet_ref, acc):
    slots, parts, peers = tiles_ref.shape[0], own_ref.shape[0], packet_ref.shape[0]
    half = row_seg_ref.shape[0] // CORES
    acc[...] = jnp.zeros_like(acc)
    count = count_ref[...]

    def block(step, _):
        results = []
        for u in range(UNROLL):
            n = step * UNROLL + u
            core, place = by_core(rows_ref[n], parts)
            product = lax.dot_general(row_seg_ref[core * half + place], tiles_ref[n], (((1,), (0,)), ((), ())), preferred_element_type=F32)
            results.append((cols_ref[n], jnp.where(n < count, product, 0.0)))
        for c, product in results:
            acc[c] += product
        return 0

    lax.fori_loop(0, slots // UNROLL, block, 0)
    packet_ref[:, :parts] = jnp.broadcast_to(own_ref[...][None], (peers,) + own_ref.shape)
    packet_ref[:, parts:] = acc[...].astype(BF16).reshape((peers,) + own_ref.shape)


def direct_kernel(rows_ref, cols_ref, count_ref, tiles_ref, packet_ref, keep_ref, send_ref, row_sum_ref, acc):
    slots, half, parts = tiles_ref.shape[0], keep_ref.shape[0], row_sum_ref.shape[0]
    acc[...] = jnp.zeros_like(acc)
    count, mine = count_ref[...], lax.axis_index(CORE)

    def block(step, _):
        results = []
        for u in range(UNROLL):
            n = step * UNROLL + u
            col = cols_ref[n]
            picked = packet_ref[col >> (parts.bit_length() - 1), col & (parts - 1)]
            product = lax.dot_general(picked, tiles_ref[n], (((1,), (1,)), ((), ())), preferred_element_type=F32)
            core, place = by_core(rows_ref[n], parts)
            results.append(((core ^ mine) * half + place, jnp.where(n < count, product, 0.0)))
        for r, product in results:
            acc[r] += product
        return 0

    lax.fori_loop(0, slots // UNROLL, block, 0)
    keep_ref[...] = acc[:half]
    send_ref[...] = acc[half:2 * half].astype(BF16)
    for h in range(parts):
        row_sum_ref[h] = jnp.sum(packet_ref[:, parts + h].astype(F32), axis=0)


def half_kernel(keep_ref, recv_ref, out_ref):
    out_ref[...] = (keep_ref[...] + recv_ref[...].astype(F32)).astype(BF16)


def image_kernel(row_sum_ref, near_recv_ref, image_ref, *next_refs):
    parts, width = row_sum_ref.shape[0], row_sum_ref.shape[-1]
    for h in range(parts):
        value = (row_sum_ref[h] + jnp.sum(near_recv_ref[:, h].astype(F32), axis=0)).astype(image_ref.dtype)
        image_ref[:, h * width:(h + 1) * width] = value
        if next_refs:
            own_ref, copies_ref = next_refs
            own_ref[h] = value
            copies_ref[:, h] = jnp.broadcast_to(value[None], (copies_ref.shape[0],) + value.shape)


def call(kernel, name, in_specs, shapes, scratch, flops, moved, *args):
    return pl.pallas_call(
        kernel,
        out_shape=tuple(jax.ShapeDtypeStruct(s, d) for s, d in shapes),
        in_specs=in_specs,
        out_specs=(VMEM,) * len(shapes),
        scratch_shapes=scratch,
        compiler_params=pltpu.CompilerParams(vmem_limit_bytes=12 * 1024 * 1024),
        cost_estimate=pl.CostEstimate(flops=flops, bytes_accessed=moved, transcendentals=0),
        name=name,
    )(*args)


def per_device(tile_values, tile_rows, tile_cols, tile_count, vectors):
    tiles = tile_values[0, 0]
    rows, cols = tile_rows[0, 0], tile_cols[0, 0]
    slots, tile = tiles.shape[0], tiles.shape[-1]
    vec_count, slice_len = vectors.shape
    parts = slice_len // tile
    peers, near = lax.axis_size(ROW), lax.axis_size(NEAR)
    piece = (parts, vec_count, tile)
    half = (near * parts, vec_count, tile)
    packets = (peers, 2 * parts, vec_count, tile)
    flops, moved = 2 * slots * vec_count * tile * tile, 2 * tiles.size
    acc = lambda n: [pltpu.VMEM((n, vec_count, tile), F32)]

    def image(own, near_copies, dtype, again):
        near_recv = lax.all_to_all(near_copies, NEAR, 0, 0)
        row_seg = lax.all_gather(near_recv.reshape(half), CORE, axis=0, tiled=True)
        (packet,) = call(
            mirror_kernel, "mirror_products", [SMEM] * 2 + [VMEM] * 4,
            [(packets, BF16)], acc(peers * parts), flops, moved, rows, cols, count, tiles, row_seg, own)
        packet = lax.all_to_all(packet, ROW, 0, 0)
        keep, send, row_sum = call(
            direct_kernel, "direct_products", [SMEM] * 2 + [VMEM] * 3,
            [(half, F32), (half, BF16), (piece, F32)], acc(CORES * half[0]), flops, moved, rows, cols, count, tiles, packet)
        recv = lax.ppermute(send, CORE, [(0, 1), (1, 0)])
        (chip,) = call(half_kernel, "chip_sum", [VMEM] * 2, [(half, BF16)], [], keep.size, 8 * keep.size, keep, recv)
        near_recv = lax.all_to_all(chip.reshape((near,) + piece), NEAR, 0, 0)
        shapes = [((vec_count, slice_len), dtype)]
        if again:
            shapes += [(piece, dtype), ((near,) + piece, dtype)]
        return call(image_kernel, "image", [VMEM] * 2, shapes, [], near_recv.size, 4 * near_recv.size, row_sum, near_recv)

    own, copies, count = call(
        start_kernel, "start", [VMEM] * 2, [(piece, BF16), ((near,) + piece, BF16), ((vec_count, tile), jnp.int32)],
        [], vectors.size, 40 * vectors.size, vectors, tile_count)
    first_image, own, copies = image(own, copies, BF16, True)
    (second_image,) = image(own, copies, F32, False)
    return (first_image, second_image)


def solution(mesh):
    rows, cols = mesh.devices.shape
    split = Mesh(mesh.devices.reshape(rows, cols // CORES, CORES), (ROW, NEAR, CORE))
    col = (NEAR, CORE)
    whole = (ROW,) + col
    return jax.shard_map(
        per_device,
        mesh=split,
        in_specs=(P(ROW, col, None, None, None), P(ROW, col, None), P(ROW, col, None), P(ROW, col), P(None, whole)),
        out_specs=(P(None, whole), P(None, whole)),
        check_vma=False,
    )
```

```python
import jax
import jax.numpy as jnp
from jax import lax
from jax.experimental import pallas as pl
from jax.experimental.pallas import tpu as pltpu
from jax.sharding import Mesh
from jax.sharding import PartitionSpec as P

UNROLL = 32
TILE_COPIES = 4
F32 = jnp.float32
BF16 = jnp.bfloat16
ROW, NEAR, CORE = "row", "near", "core"
CORES = 2
VMEM = pl.BlockSpec(memory_space=pltpu.VMEM)
SMEM = pl.BlockSpec(memory_space=pltpu.SMEM)
ANY = pl.BlockSpec(memory_space=pl.ANY)


def by_core(tile_row, parts):
    part, owner = tile_row & (parts - 1), tile_row >> (parts.bit_length() - 1)
    return owner & (CORES - 1), (owner >> (CORES.bit_length() - 1)) * parts + part


def start_kernel(vectors_in, rows_in, cols_in, tiles_in, count_ref, own_ref, copies_ref, counts_ref, rows_ref, cols_ref, tiles_ref, vectors_ref, arrived):
    chunk = tiles_ref.shape[0] // TILE_COPIES
    spans = [pl.ds(i * chunk, chunk) for i in range(TILE_COPIES)]
    moves = [(vectors_in, vectors_ref), (rows_in, rows_ref), (cols_in, cols_ref)] + [(tiles_in.at[s], tiles_ref.at[s]) for s in spans]
    copies = [pltpu.make_async_copy(source, target, arrived.at[i]) for i, (source, target) in enumerate(moves)]
    for copy in copies:
        copy.start()
    counts_ref[...] = jnp.broadcast_to(count_ref[...], counts_ref.shape)
    copies[0].wait()
    width = own_ref.shape[-1]
    for h in range(own_ref.shape[0]):
        value = vectors_ref[:, h * width:(h + 1) * width]
        own_ref[h] = value
        copies_ref[:, h] = jnp.broadcast_to(value[None], (copies_ref.shape[0],) + value.shape)
    for copy in copies[1:]:
        copy.wait()


def mirror_kernel(rows_ref, cols_ref, count_ref, tiles_ref, row_seg_ref, own_ref, packet_ref, acc):
    slots, parts, peers = tiles_ref.shape[0], own_ref.shape[0], packet_ref.shape[0]
    half = row_seg_ref.shape[0] // CORES
    acc[...] = jnp.zeros_like(acc)
    count = count_ref[...]

    def block(step, _):
        results = []
        for u in range(UNROLL):
            n = step * UNROLL + u
            core, place = by_core(rows_ref[n], parts)
            product = lax.dot_general(row_seg_ref[core * half + place], tiles_ref[n], (((1,), (0,)), ((), ())), preferred_element_type=F32)
            results.append((cols_ref[n], jnp.where(n < count, product, 0.0)))
        for c, product in results:
            acc[c] += product
        return 0

    lax.fori_loop(0, slots // UNROLL, block, 0)
    packet_ref[:, :parts] = jnp.broadcast_to(own_ref[...][None], (peers,) + own_ref.shape)
    packet_ref[:, parts:] = acc[...].astype(BF16).reshape((peers,) + own_ref.shape)


def direct_kernel(rows_ref, cols_ref, count_ref, tiles_ref, packet_ref, keep_ref, send_ref, row_sum_ref, acc):
    slots, half, parts = tiles_ref.shape[0], keep_ref.shape[0], row_sum_ref.shape[0]
    acc[...] = jnp.zeros_like(acc)
    count, mine = count_ref[...], lax.axis_index(CORE)

    def block(step, _):
        results = []
        for u in range(UNROLL):
            n = step * UNROLL + u
            col = cols_ref[n]
            picked = packet_ref[col >> (parts.bit_length() - 1), col & (parts - 1)]
            product = lax.dot_general(picked, tiles_ref[n], (((1,), (1,)), ((), ())), preferred_element_type=F32)
            core, place = by_core(rows_ref[n], parts)
            results.append(((core ^ mine) * half + place, jnp.where(n < count, product, 0.0)))
        for r, product in results:
            acc[r] += product
        return 0

    lax.fori_loop(0, slots // UNROLL, block, 0)
    keep_ref[...] = acc[:half]
    send_ref[...] = acc[half:2 * half].astype(BF16)
    for h in range(parts):
        row_sum_ref[h] = jnp.sum(packet_ref[:, parts + h].astype(F32), axis=0)


def half_kernel(keep_ref, recv_ref, out_ref):
    other = CORES - 1 - lax.axis_index(CORE)
    out_ref[...] = (keep_ref[...] + recv_ref[other].astype(F32)).astype(BF16)


def image_kernel(row_sum_ref, near_recv_ref, image_ref, *next_refs):
    parts, width = row_sum_ref.shape[0], row_sum_ref.shape[-1]
    for h in range(parts):
        value = (row_sum_ref[h] + jnp.sum(near_recv_ref[:, h].astype(F32), axis=0)).astype(image_ref.dtype)
        image_ref[:, h * width:(h + 1) * width] = value
        if next_refs:
            own_ref, copies_ref = next_refs
            own_ref[h] = value
            copies_ref[:, h] = jnp.broadcast_to(value[None], (copies_ref.shape[0],) + value.shape)


def call(kernel, name, in_specs, shapes, scratch, flops, moved, *args, vmem=12 * 1024):
    return pl.pallas_call(
        kernel,
        out_shape=tuple(jax.ShapeDtypeStruct(s, d) for s, d in shapes),
        in_specs=in_specs,
        out_specs=(VMEM,) * len(shapes),
        scratch_shapes=scratch,
        compiler_params=pltpu.CompilerParams(vmem_limit_bytes=vmem * 1024),
        cost_estimate=pl.CostEstimate(flops=flops, bytes_accessed=moved, transcendentals=0),
        name=name,
    )(*args)


def per_device(tile_values, tile_rows, tile_cols, tile_count, vectors):
    tiles = tile_values[0, 0]
    slots, tile = tiles.shape[0], tiles.shape[-1]
    vec_count, slice_len = vectors.shape
    parts = slice_len // tile
    peers, near = lax.axis_size(ROW), lax.axis_size(NEAR)
    piece = (parts, vec_count, tile)
    half = (near * parts, vec_count, tile)
    packets = (peers, 2 * parts, vec_count, tile)
    flops, moved = 2 * slots * vec_count * tile * tile, 2 * tiles.size
    acc = lambda n: [pltpu.VMEM((n, vec_count, tile), F32)]

    def image(own, near_copies, dtype, again):
        near_recv = lax.all_to_all(near_copies, NEAR, 0, 0)
        row_seg = lax.all_gather(near_recv.reshape(half), CORE, axis=0, tiled=True)
        (packet,) = call(
            mirror_kernel, "mirror_products", [SMEM] * 2 + [VMEM] * 4,
            [(packets, BF16)], acc(peers * parts), flops, moved, rows, cols, count, tiles, row_seg, own)
        packet = lax.all_to_all(packet, ROW, 0, 0)
        keep, send, row_sum = call(
            direct_kernel, "direct_products", [SMEM] * 2 + [VMEM] * 3,
            [(half, F32), (half, BF16), (piece, F32)], acc(CORES * half[0]), flops, moved, rows, cols, count, tiles, packet)
        recv = lax.all_gather(send, CORE, axis=0)
        (chip,) = call(half_kernel, "chip_sum", [VMEM] * 2, [(half, BF16)], [], keep.size, 8 * keep.size, keep, recv)
        near_recv = lax.all_to_all(chip.reshape((near,) + piece), NEAR, 0, 0)
        shapes = [((vec_count, slice_len), dtype)]
        if again:
            shapes += [(piece, dtype), ((near,) + piece, dtype)]
        return call(image_kernel, "image", [VMEM] * 2, shapes, [], near_recv.size, 4 * near_recv.size, row_sum, near_recv)

    places = [(tile_rows.shape, jnp.int32), (tile_cols.shape, jnp.int32)]
    own, copies, count, rows, cols, tiles = call(
        start_kernel, "start", [ANY] * 4 + [VMEM],
        [(piece, BF16), ((near,) + piece, BF16), ((vec_count, tile), jnp.int32)] + places + [(tiles.shape, BF16)],
        [pltpu.VMEM(vectors.shape, BF16), pltpu.SemaphoreType.DMA((3 + TILE_COPIES,))], vectors.size, moved,
        vectors, tile_rows, tile_cols, tiles, tile_count, vmem=50500)
    rows, cols = rows[0, 0], cols[0, 0]
    first_image, own, copies = image(own, copies, BF16, True)
    (second_image,) = image(own, copies, F32, False)
    return (first_image, second_image)


def solution(mesh):
    rows, cols = mesh.devices.shape
    split = Mesh(mesh.devices.reshape(rows, cols // CORES, CORES), (ROW, NEAR, CORE))
    col = (NEAR, CORE)
    whole = (ROW,) + col
    return jax.shard_map(
        per_device,
        mesh=split,
        in_specs=(P(ROW, col, None, None, None), P(ROW, col, None), P(ROW, col, None), P(ROW, col), P(None, whole)),
        out_specs=(P(None, whole), P(None, whole)),
        check_vma=False,
    )
```

```python
import jax
import jax.numpy as jnp
from jax import lax
from jax.experimental import pallas as pl
from jax.experimental.pallas import tpu as pltpu
from jax.sharding import Mesh
from jax.sharding import PartitionSpec as P

UNROLL = 48
TILE_COPIES = 4
F32 = jnp.float32
BF16 = jnp.bfloat16
ROW, NEAR, CORE = "row", "near", "core"
CORES = 2
VMEM = pl.BlockSpec(memory_space=pltpu.VMEM)
SMEM = pl.BlockSpec(memory_space=pltpu.SMEM)
ANY = pl.BlockSpec(memory_space=pl.ANY)


def by_core(tile_row, parts):
    part, owner = tile_row & (parts - 1), tile_row >> (parts.bit_length() - 1)
    return owner & (CORES - 1), (owner >> (CORES.bit_length() - 1)) * parts + part


def start_kernel(vectors_in, tiles_in, places_ref, own_ref, copies_ref, places_out, tiles_ref, vectors_ref, arrived):
    chunk = tiles_ref.shape[0] // TILE_COPIES
    spans = [pl.ds(i * chunk, chunk) for i in range(TILE_COPIES)]
    moves = [(vectors_in, vectors_ref)] + [(tiles_in.at[s], tiles_ref.at[s]) for s in spans]
    copies = [pltpu.make_async_copy(source, target, arrived.at[i]) for i, (source, target) in enumerate(moves)]
    for copy in copies:
        copy.start()
    places_out[...] = places_ref[...]
    copies[0].wait()
    width = own_ref.shape[-1]
    for h in range(own_ref.shape[0]):
        value = vectors_ref[:, h * width:(h + 1) * width]
        own_ref[h] = value
        copies_ref[:, h] = jnp.broadcast_to(value[None], (copies_ref.shape[0],) + value.shape)
    for copy in copies[1:]:
        copy.wait()


def mirror_kernel(places_ref, tiles_ref, row_seg_ref, own_ref, packet_ref, acc):
    slots, parts, peers = tiles_ref.shape[0], own_ref.shape[0], packet_ref.shape[0]
    half = row_seg_ref.shape[0] // CORES
    acc[...] = jnp.zeros_like(acc)
    count, spare = places_ref[2 * slots], acc.shape[0] - 1

    def block(step, _):
        results = []
        for u in range(UNROLL):
            n = step * UNROLL + u
            core, place = by_core(places_ref[n] & (CORES * half - 1), parts)
            product = lax.dot_general(row_seg_ref[core * half + place], tiles_ref[n], (((1,), (0,)), ((), ())), preferred_element_type=F32)
            results.append((jnp.where(n < count, places_ref[slots + n], spare), product))
        for c, product in results:
            acc[c] += product
        return 0

    lax.fori_loop(0, slots // UNROLL, block, 0)
    packet_ref[:, :parts] = jnp.broadcast_to(own_ref[...][None], (peers,) + own_ref.shape)
    packet_ref[:, parts:] = acc[:peers * parts].astype(BF16).reshape((peers,) + own_ref.shape)


def direct_kernel(places_ref, tiles_ref, packet_ref, keep_ref, send_ref, row_sum_ref, acc):
    slots, half, parts = tiles_ref.shape[0], keep_ref.shape[0], row_sum_ref.shape[0]
    acc[...] = jnp.zeros_like(acc)
    count, mine, spare = places_ref[2 * slots], lax.axis_index(CORE), acc.shape[0] - 1

    def block(step, _):
        results = []
        for u in range(UNROLL):
            n = step * UNROLL + u
            col = places_ref[slots + n] & (packet_ref.shape[0] * parts - 1)
            picked = packet_ref[col >> (parts.bit_length() - 1), col & (parts - 1)]
            product = lax.dot_general(picked, tiles_ref[n], (((1,), (1,)), ((), ())), preferred_element_type=F32)
            core, place = by_core(places_ref[n], parts)
            results.append((jnp.where(n < count, (core ^ mine) * half + place, spare), product))
        for r, product in results:
            acc[r] += product
        return 0

    lax.fori_loop(0, slots // UNROLL, block, 0)
    keep_ref[...] = acc[:half]
    send_ref[...] = acc[half:2 * half].astype(BF16)
    for h in range(parts):
        row_sum_ref[h] = jnp.sum(packet_ref[:, parts + h].astype(F32), axis=0)


def half_kernel(keep_ref, recv_ref, out_ref):
    other = CORES - 1 - lax.axis_index(CORE)
    out_ref[...] = (keep_ref[...] + recv_ref[other].astype(F32)).astype(BF16)


def image_kernel(row_sum_ref, near_recv_ref, image_ref, *next_refs):
    parts, width = row_sum_ref.shape[0], row_sum_ref.shape[-1]
    for h in range(parts):
        value = (row_sum_ref[h] + jnp.sum(near_recv_ref[:, h].astype(F32), axis=0)).astype(image_ref.dtype)
        image_ref[:, h * width:(h + 1) * width] = value
        if next_refs:
            own_ref, copies_ref = next_refs
            own_ref[h] = value
            copies_ref[:, h] = jnp.broadcast_to(value[None], (copies_ref.shape[0],) + value.shape)


def call(kernel, name, in_specs, shapes, scratch, flops, moved, *args, vmem=12 * 1024):
    return pl.pallas_call(
        kernel,
        out_shape=tuple(jax.ShapeDtypeStruct(s, d) for s, d in shapes),
        in_specs=in_specs,
        out_specs=(VMEM,) * len(shapes),
        scratch_shapes=scratch,
        compiler_params=pltpu.CompilerParams(vmem_limit_bytes=vmem * 1024),
        cost_estimate=pl.CostEstimate(flops=flops, bytes_accessed=moved, transcendentals=0),
        name=name,
    )(*args)


def per_device(tile_values, tile_rows, tile_cols, tile_count, vectors):
    tiles = tile_values[0, 0]
    slots, tile = tiles.shape[0], tiles.shape[-1]
    vec_count, slice_len = vectors.shape
    parts = slice_len // tile
    peers, near = lax.axis_size(ROW), lax.axis_size(NEAR)
    piece = (parts, vec_count, tile)
    half = (near * parts, vec_count, tile)
    packets = (peers, 2 * parts, vec_count, tile)
    flops, moved = 2 * slots * vec_count * tile * tile, 2 * tiles.size
    acc = lambda n: [pltpu.VMEM((n + 1, vec_count, tile), F32)]

    def image(own, near_copies, dtype, again):
        near_recv = lax.all_to_all(near_copies, NEAR, 0, 0)
        row_seg = lax.all_gather(near_recv.reshape(half), CORE, axis=0, tiled=True)
        (packet,) = call(
            mirror_kernel, "mirror_products", [SMEM] + [VMEM] * 3,
            [(packets, BF16)], acc(peers * parts), flops, moved, places, tiles, row_seg, own)
        packet = lax.all_to_all(packet, ROW, 0, 0)
        keep, send, row_sum = call(
            direct_kernel, "direct_products", [SMEM] + [VMEM] * 2,
            [(half, F32), (half, BF16), (piece, F32)], acc(CORES * half[0]), flops, moved, places, tiles, packet)
        recv = lax.all_gather(send, CORE, axis=0)
        (chip,) = call(half_kernel, "chip_sum", [VMEM] * 2, [(half, BF16)], [], keep.size, 8 * keep.size, keep, recv)
        near_recv = lax.all_to_all(chip.reshape((near,) + piece), NEAR, 0, 0)
        shapes = [((vec_count, slice_len), dtype)]
        if again:
            shapes += [(piece, dtype), ((near,) + piece, dtype)]
        return call(image_kernel, "image", [VMEM] * 2, shapes, [], near_recv.size, 4 * near_recv.size, row_sum, near_recv)

    places = jnp.concatenate([tile_rows[0, 0], tile_cols[0, 0], tile_count[0]])
    own, copies, places, tiles = call(
        start_kernel, "start", [ANY] * 2 + [VMEM],
        [(piece, BF16), ((near,) + piece, BF16), (places.shape, jnp.int32), (tiles.shape, BF16)],
        [pltpu.VMEM(vectors.shape, BF16), pltpu.SemaphoreType.DMA((1 + TILE_COPIES,))], vectors.size, moved,
        vectors, tiles, places, vmem=50500)
    first_image, own, copies = image(own, copies, BF16, True)
    (second_image,) = image(own, copies, F32, False)
    return (first_image, second_image)


def solution(mesh):
    rows, cols = mesh.devices.shape
    split = Mesh(mesh.devices.reshape(rows, cols // CORES, CORES), (ROW, NEAR, CORE))
    col = (NEAR, CORE)
    whole = (ROW,) + col
    return jax.shard_map(
        per_device,
        mesh=split,
        in_specs=(P(ROW, col, None, None, None), P(ROW, col, None), P(ROW, col, None), P(ROW, col), P(None, whole)),
        out_specs=(P(None, whole), P(None, whole)),
        check_vma=False,
    )
```

```python
import jax
import jax.numpy as jnp
from jax import lax
from jax.experimental import pallas as pl
from jax.experimental.pallas import tpu as pltpu
from jax.sharding import Mesh
from jax.sharding import PartitionSpec as P

UNROLL = 48
TILE_COPIES = 4
F32 = jnp.float32
BF16 = jnp.bfloat16
ROW, NEAR, CORE = "row", "near", "core"
CORES = 2
VMEM = pl.BlockSpec(memory_space=pltpu.VMEM)
SMEM = pl.BlockSpec(memory_space=pltpu.SMEM)
ANY = pl.BlockSpec(memory_space=pl.ANY)


def by_core(tile_row, parts):
    part, owner = tile_row & (parts - 1), tile_row >> (parts.bit_length() - 1)
    return owner & (CORES - 1), (owner >> (CORES.bit_length() - 1)) * parts + part


def start_kernel(vectors_ref, own_ref, copies_ref):
    width = own_ref.shape[-1]
    for h in range(own_ref.shape[0]):
        value = vectors_ref[:, h * width:(h + 1) * width]
        own_ref[h] = value
        copies_ref[:, h] = jnp.broadcast_to(value[None], (copies_ref.shape[0],) + value.shape)


def load_kernel(tiles_in, places_ref, places_out, tiles_ref, arrived):
    chunk = tiles_ref.shape[0] // TILE_COPIES
    spans = [pl.ds(i * chunk, chunk) for i in range(TILE_COPIES)]
    copies = [pltpu.make_async_copy(tiles_in.at[s], tiles_ref.at[s], arrived.at[i]) for i, s in enumerate(spans)]
    for copy in copies:
        copy.start()
    places_out[...] = places_ref[...]
    for copy in copies:
        copy.wait()


def mirror_kernel(places_ref, tiles_ref, row_seg_ref, own_ref, packet_ref, acc):
    slots, parts, peers = tiles_ref.shape[0], own_ref.shape[0], packet_ref.shape[0]
    half = row_seg_ref.shape[0] // CORES
    acc[...] = jnp.zeros_like(acc)
    count, spare = places_ref[2 * slots], acc.shape[0] - 1

    def block(step, _):
        results = []
        for u in range(UNROLL):
            n = step * UNROLL + u
            core, place = by_core(places_ref[n] & (CORES * half - 1), parts)
            product = lax.dot_general(row_seg_ref[core * half + place], tiles_ref[n], (((1,), (0,)), ((), ())), preferred_element_type=F32)
            results.append((jnp.where(n < count, places_ref[slots + n], spare), product))
        for c, product in results:
            acc[c] += product
        return 0

    lax.fori_loop(0, slots // UNROLL, block, 0)
    packet_ref[:, :parts] = jnp.broadcast_to(own_ref[...][None], (peers,) + own_ref.shape)
    packet_ref[:, parts:] = acc[:peers * parts].astype(BF16).reshape((peers,) + own_ref.shape)


def direct_kernel(places_ref, tiles_ref, packet_ref, keep_ref, send_ref, row_sum_ref, acc):
    slots, half, parts = tiles_ref.shape[0], keep_ref.shape[0], row_sum_ref.shape[0]
    acc[...] = jnp.zeros_like(acc)
    count, mine, spare = places_ref[2 * slots], lax.axis_index(CORE), acc.shape[0] - 1

    def block(step, _):
        results = []
        for u in range(UNROLL):
            n = step * UNROLL + u
            col = places_ref[slots + n] & (packet_ref.shape[0] * parts - 1)
            picked = packet_ref[col >> (parts.bit_length() - 1), col & (parts - 1)]
            product = lax.dot_general(picked, tiles_ref[n], (((1,), (1,)), ((), ())), preferred_element_type=F32)
            core, place = by_core(places_ref[n], parts)
            results.append((jnp.where(n < count, (core ^ mine) * half + place, spare), product))
        for r, product in results:
            acc[r] += product
        return 0

    lax.fori_loop(0, slots // UNROLL, block, 0)
    keep_ref[...] = acc[:half]
    send_ref[...] = acc[half:2 * half].astype(BF16)
    for h in range(parts):
        row_sum_ref[h] = jnp.sum(packet_ref[:, parts + h].astype(F32), axis=0)


def half_kernel(keep_ref, recv_ref, out_ref):
    other = CORES - 1 - lax.axis_index(CORE)
    out_ref[...] = (keep_ref[...] + recv_ref[other].astype(F32)).astype(BF16)


def image_kernel(row_sum_ref, near_recv_ref, image_ref, *next_refs):
    parts, width = row_sum_ref.shape[0], row_sum_ref.shape[-1]
    for h in range(parts):
        value = (row_sum_ref[h] + jnp.sum(near_recv_ref[:, h].astype(F32), axis=0)).astype(image_ref.dtype)
        image_ref[:, h * width:(h + 1) * width] = value
        if next_refs:
            own_ref, copies_ref = next_refs
            own_ref[h] = value
            copies_ref[:, h] = jnp.broadcast_to(value[None], (copies_ref.shape[0],) + value.shape)


def call(kernel, name, in_specs, shapes, scratch, flops, moved, *args, vmem=12 * 1024):
    return pl.pallas_call(
        kernel,
        out_shape=tuple(jax.ShapeDtypeStruct(s, d) for s, d in shapes),
        in_specs=in_specs,
        out_specs=(VMEM,) * len(shapes),
        scratch_shapes=scratch,
        compiler_params=pltpu.CompilerParams(vmem_limit_bytes=vmem * 1024),
        cost_estimate=pl.CostEstimate(flops=flops, bytes_accessed=moved, transcendentals=0),
        name=name,
    )(*args)


def per_device(tile_values, tile_rows, tile_cols, tile_count, vectors):
    tiles = tile_values[0, 0]
    slots, tile = tiles.shape[0], tiles.shape[-1]
    vec_count, slice_len = vectors.shape
    parts = slice_len // tile
    peers, near = lax.axis_size(ROW), lax.axis_size(NEAR)
    piece = (parts, vec_count, tile)
    half = (near * parts, vec_count, tile)
    packets = (peers, 2 * parts, vec_count, tile)
    flops, moved = 2 * slots * vec_count * tile * tile, 2 * tiles.size
    acc = lambda n: [pltpu.VMEM((n + 1, vec_count, tile), F32)]

    def image(own, near_copies, dtype, again):
        near_recv = lax.all_to_all(near_copies, NEAR, 0, 0)
        row_seg = lax.all_gather(near_recv.reshape(half), CORE, axis=0, tiled=True)
        (packet,) = call(
            mirror_kernel, "mirror_products", [SMEM] + [VMEM] * 3,
            [(packets, BF16)], acc(peers * parts), flops, moved, places, tiles, row_seg, own)
        packet = lax.all_to_all(packet, ROW, 0, 0)
        keep, send, row_sum = call(
            direct_kernel, "direct_products", [SMEM] + [VMEM] * 2,
            [(half, F32), (half, BF16), (piece, F32)], acc(CORES * half[0]), flops, moved, places, tiles, packet)
        recv = lax.all_gather(send, CORE, axis=0)
        (chip,) = call(half_kernel, "chip_sum", [VMEM] * 2, [(half, BF16)], [], keep.size, 8 * keep.size, keep, recv)
        near_recv = lax.all_to_all(chip.reshape((near,) + piece), NEAR, 0, 0)
        shapes = [((vec_count, slice_len), dtype)]
        if again:
            shapes += [(piece, dtype), ((near,) + piece, dtype)]
        return call(image_kernel, "image", [VMEM] * 2, shapes, [], near_recv.size, 4 * near_recv.size, row_sum, near_recv)

    places = jnp.concatenate([tile_rows[0, 0], tile_cols[0, 0], tile_count[0]])
    places, tiles = call(
        load_kernel, "load", [ANY, VMEM], [(places.shape, jnp.int32), (tiles.shape, BF16)],
        [pltpu.SemaphoreType.DMA((TILE_COPIES,))], vectors.size, 2 * moved, tiles, places, vmem=50500)
    own, copies = call(
        start_kernel, "start", [VMEM], [(piece, BF16), ((near,) + piece, BF16)], [], vectors.size, 40 * vectors.size, vectors)
    first_image, own, copies = image(own, copies, BF16, True)
    (second_image,) = image(own, copies, F32, False)
    return (first_image, second_image)


def solution(mesh):
    rows, cols = mesh.devices.shape
    split = Mesh(mesh.devices.reshape(rows, cols // CORES, CORES), (ROW, NEAR, CORE))
    col = (NEAR, CORE)
    whole = (ROW,) + col
    return jax.shard_map(
        per_device,
        mesh=split,
        in_specs=(P(ROW, col, None, None, None), P(ROW, col, None), P(ROW, col, None), P(ROW, col), P(None, whole)),
        out_specs=(P(None, whole), P(None, whole)),
        check_vma=False,
    )
```

```python
import jax
import jax.numpy as jnp
from jax import lax
from jax.experimental import pallas as pl
from jax.experimental.pallas import tpu as pltpu
from jax.sharding import Mesh
from jax.sharding import PartitionSpec as P

UNROLL = 96
TILE_COPIES = 4
F32 = jnp.float32
BF16 = jnp.bfloat16
ROW, NEAR, CORE = "row", "near", "core"
CORES = 2
VMEM = pl.BlockSpec(memory_space=pltpu.VMEM)
SMEM = pl.BlockSpec(memory_space=pltpu.SMEM)
ANY = pl.BlockSpec(memory_space=pl.ANY)


def by_core(tile_row, parts):
    part, owner = tile_row & (parts - 1), tile_row >> (parts.bit_length() - 1)
    return owner & (CORES - 1), (owner >> (CORES.bit_length() - 1)) * parts + part


def start_kernel(vectors_ref, own_ref, copies_ref):
    width = own_ref.shape[-1]
    for h in range(own_ref.shape[0]):
        value = vectors_ref[:, h * width:(h + 1) * width]
        own_ref[h] = value
        copies_ref[:, h] = jnp.broadcast_to(value[None], (copies_ref.shape[0],) + value.shape)


def load_kernel(tiles_in, places_ref, places_out, tiles_ref, arrived):
    chunk = tiles_ref.shape[0] // TILE_COPIES
    spans = [pl.ds(i * chunk, chunk) for i in range(TILE_COPIES)]
    copies = [pltpu.make_async_copy(tiles_in.at[s], tiles_ref.at[s], arrived.at[i]) for i, s in enumerate(spans)]
    for copy in copies:
        copy.start()
    places_out[...] = places_ref[...]
    for copy in copies:
        copy.wait()


def mirror_kernel(places_ref, tiles_ref, row_seg_ref, own_ref, packet_ref, acc):
    slots, parts, peers = tiles_ref.shape[0], own_ref.shape[0], packet_ref.shape[0]
    half = row_seg_ref.shape[0] // CORES
    acc[...] = jnp.zeros_like(acc)
    count, spare = places_ref[2 * slots], acc.shape[0] - 1

    def block(step, _):
        results = []
        for u in range(UNROLL):
            n = step * UNROLL + u
            core, place = by_core(places_ref[n] & (CORES * half - 1), parts)
            product = lax.dot_general(row_seg_ref[core * half + place], tiles_ref[n], (((1,), (0,)), ((), ())), preferred_element_type=F32)
            results.append((jnp.where(n < count, places_ref[slots + n], spare), product))
        for c, product in results:
            acc[c] += product
        return 0

    lax.fori_loop(0, slots // UNROLL, block, 0)
    packet_ref[:, :parts] = jnp.broadcast_to(own_ref[...][None], (peers,) + own_ref.shape)
    packet_ref[:, parts:] = acc[:peers * parts].astype(BF16).reshape((peers,) + own_ref.shape)


def direct_kernel(places_ref, tiles_ref, packet_ref, keep_ref, send_ref, row_sum_ref, acc):
    slots, half, parts = tiles_ref.shape[0], keep_ref.shape[0], row_sum_ref.shape[0]
    acc[...] = jnp.zeros_like(acc)
    count, mine, spare = places_ref[2 * slots], lax.axis_index(CORE), acc.shape[0] - 1

    def block(step, _):
        results = []
        for u in range(UNROLL):
            n = step * UNROLL + u
            col = places_ref[slots + n] & (packet_ref.shape[0] * parts - 1)
            picked = packet_ref[col >> (parts.bit_length() - 1), col & (parts - 1)]
            product = lax.dot_general(picked, tiles_ref[n], (((1,), (1,)), ((), ())), preferred_element_type=F32)
            core, place = by_core(places_ref[n], parts)
            results.append((jnp.where(n < count, (core ^ mine) * half + place, spare), product))
        for r, product in results:
            acc[r] += product
        return 0

    lax.fori_loop(0, slots // UNROLL, block, 0)
    keep_ref[...] = acc[:half]
    send_ref[...] = acc[half:2 * half].astype(BF16)
    for h in range(parts):
        row_sum_ref[h] = jnp.sum(packet_ref[:, parts + h].astype(F32), axis=0)


def half_kernel(keep_ref, recv_ref, out_ref):
    other = CORES - 1 - lax.axis_index(CORE)
    out_ref[...] = (keep_ref[...] + recv_ref[other].astype(F32)).astype(BF16)


def image_kernel(row_sum_ref, near_recv_ref, image_ref, *next_refs):
    parts, width = row_sum_ref.shape[0], row_sum_ref.shape[-1]
    for h in range(parts):
        value = (row_sum_ref[h] + jnp.sum(near_recv_ref[:, h].astype(F32), axis=0)).astype(image_ref.dtype)
        image_ref[:, h * width:(h + 1) * width] = value
        if next_refs:
            own_ref, copies_ref = next_refs
            own_ref[h] = value
            copies_ref[:, h] = jnp.broadcast_to(value[None], (copies_ref.shape[0],) + value.shape)


def call(kernel, name, in_specs, shapes, scratch, flops, moved, *args, vmem=12 * 1024):
    return pl.pallas_call(
        kernel,
        out_shape=tuple(jax.ShapeDtypeStruct(s, d) for s, d in shapes),
        in_specs=in_specs,
        out_specs=(VMEM,) * len(shapes),
        scratch_shapes=scratch,
        compiler_params=pltpu.CompilerParams(vmem_limit_bytes=vmem * 1024),
        cost_estimate=pl.CostEstimate(flops=flops, bytes_accessed=moved, transcendentals=0),
        name=name,
    )(*args)


def per_device(tile_values, tile_rows, tile_cols, tile_count, vectors):
    tiles = tile_values[0, 0]
    slots, tile = tiles.shape[0], tiles.shape[-1]
    vec_count, slice_len = vectors.shape
    parts = slice_len // tile
    peers, near = lax.axis_size(ROW), lax.axis_size(NEAR)
    piece = (parts, vec_count, tile)
    half = (near * parts, vec_count, tile)
    packets = (peers, 2 * parts, vec_count, tile)
    flops, moved = 2 * slots * vec_count * tile * tile, 2 * tiles.size
    acc = lambda n: [pltpu.VMEM((n + 1, vec_count, tile), F32)]

    def image(own, near_copies, dtype, again):
        near_recv = lax.all_to_all(near_copies, NEAR, 0, 0)
        row_seg = lax.all_gather(near_recv.reshape(half), CORE, axis=0, tiled=True)
        (packet,) = call(
            mirror_kernel, "mirror_products", [SMEM] + [VMEM] * 3,
            [(packets, BF16)], acc(peers * parts), flops, moved, places, tiles, row_seg, own)
        packet = lax.all_to_all(packet, ROW, 0, 0)
        keep, send, row_sum = call(
            direct_kernel, "direct_products", [SMEM] + [VMEM] * 2,
            [(half, F32), (half, BF16), (piece, F32)], acc(CORES * half[0]), flops, moved, places, tiles, packet)
        recv = lax.all_gather(send, CORE, axis=0)
        (chip,) = call(half_kernel, "chip_sum", [VMEM] * 2, [(half, BF16)], [], keep.size, 8 * keep.size, keep, recv)
        near_recv = lax.all_to_all(chip.reshape((near,) + piece), NEAR, 0, 0)
        shapes = [((vec_count, slice_len), dtype)]
        if again:
            shapes += [(piece, dtype), ((near,) + piece, dtype)]
        return call(image_kernel, "image", [VMEM] * 2, shapes, [], near_recv.size, 4 * near_recv.size, row_sum, near_recv)

    places = jnp.concatenate([tile_rows[0, 0], tile_cols[0, 0], tile_count[0]])
    places, tiles = call(
        load_kernel, "load", [ANY, VMEM], [(places.shape, jnp.int32), (tiles.shape, BF16)],
        [pltpu.SemaphoreType.DMA((TILE_COPIES,))], vectors.size, 2 * moved, tiles, places, vmem=50500)
    own, copies = call(
        start_kernel, "start", [VMEM], [(piece, BF16), ((near,) + piece, BF16)], [], vectors.size, 40 * vectors.size, vectors, vmem=57000)
    first_image, own, copies = image(own, copies, BF16, True)
    (second_image,) = image(own, copies, F32, False)
    return (first_image, second_image)


def solution(mesh):
    rows, cols = mesh.devices.shape
    split = Mesh(mesh.devices.reshape(rows, cols // CORES, CORES), (ROW, NEAR, CORE))
    col = (NEAR, CORE)
    whole = (ROW,) + col
    return jax.shard_map(
        per_device,
        mesh=split,
        in_specs=(P(ROW, col, None, None, None), P(ROW, col, None), P(ROW, col, None), P(ROW, col), P(None, whole)),
        out_specs=(P(None, whole), P(None, whole)),
        check_vma=False,
    )
```

```python
import jax
import jax.numpy as jnp
from jax import lax
from jax.experimental import pallas as pl
from jax.experimental.pallas import tpu as pltpu
from jax.sharding import Mesh
from jax.sharding import PartitionSpec as P

UNROLL = 96
LAG = 16
TILE_COPIES = 4
F32 = jnp.float32
BF16 = jnp.bfloat16
ROW, NEAR, CORE = "row", "near", "core"
CORES = 2
VMEM = pl.BlockSpec(memory_space=pltpu.VMEM)
SMEM = pl.BlockSpec(memory_space=pltpu.SMEM)
ANY = pl.BlockSpec(memory_space=pl.ANY)


def by_core(tile_row, parts):
    part, owner = tile_row & (parts - 1), tile_row >> (parts.bit_length() - 1)
    return owner & (CORES - 1), (owner >> (CORES.bit_length() - 1)) * parts + part


def start_kernel(vectors_ref, own_ref, copies_ref):
    width = own_ref.shape[-1]
    for h in range(own_ref.shape[0]):
        value = vectors_ref[:, h * width:(h + 1) * width]
        own_ref[h] = value
        copies_ref[:, h] = jnp.broadcast_to(value[None], (copies_ref.shape[0],) + value.shape)


def load_kernel(tiles_in, places_ref, places_out, tiles_ref, arrived):
    chunk = tiles_ref.shape[0] // TILE_COPIES
    spans = [pl.ds(i * chunk, chunk) for i in range(TILE_COPIES)]
    copies = [pltpu.make_async_copy(tiles_in.at[s], tiles_ref.at[s], arrived.at[i]) for i, s in enumerate(spans)]
    for copy in copies:
        copy.start()
    places_out[...] = places_ref[...]
    for copy in copies:
        copy.wait()


def add(acc, result):
    where, product = result
    acc[where] += product


def mirror_kernel(places_ref, tiles_ref, row_seg_ref, own_ref, packet_ref, acc):
    slots, parts, peers = tiles_ref.shape[0], own_ref.shape[0], packet_ref.shape[0]
    half = row_seg_ref.shape[0] // CORES
    acc[...] = jnp.zeros_like(acc)
    count, spare = places_ref[2 * slots], acc.shape[0] - 1

    def block(step, _):
        results = []
        for u in range(UNROLL):
            n = step * UNROLL + u
            core, place = by_core(places_ref[n] & (CORES * half - 1), parts)
            product = lax.dot_general(row_seg_ref[core * half + place], tiles_ref[n], (((1,), (0,)), ((), ())), preferred_element_type=F32)
            results.append((jnp.where(n < count, places_ref[slots + n], spare), product))
            if u >= LAG:
                add(acc, results.pop(0))
        for result in results:
            add(acc, result)
        return 0

    lax.fori_loop(0, slots // UNROLL, block, 0)
    packet_ref[:, :parts] = jnp.broadcast_to(own_ref[...][None], (peers,) + own_ref.shape)
    packet_ref[:, parts:] = acc[:peers * parts].astype(BF16).reshape((peers,) + own_ref.shape)


def direct_kernel(places_ref, tiles_ref, packet_ref, keep_ref, send_ref, row_sum_ref, acc):
    slots, half, parts = tiles_ref.shape[0], keep_ref.shape[0], row_sum_ref.shape[0]
    acc[...] = jnp.zeros_like(acc)
    count, mine, spare = places_ref[2 * slots], lax.axis_index(CORE), acc.shape[0] - 1

    def block(step, _):
        results = []
        for u in range(UNROLL):
            n = step * UNROLL + u
            col = places_ref[slots + n] & (packet_ref.shape[0] * parts - 1)
            picked = packet_ref[col >> (parts.bit_length() - 1), col & (parts - 1)]
            product = lax.dot_general(picked, tiles_ref[n], (((1,), (1,)), ((), ())), preferred_element_type=F32)
            core, place = by_core(places_ref[n], parts)
            results.append((jnp.where(n < count, (core ^ mine) * half + place, spare), product))
            if u >= LAG:
                add(acc, results.pop(0))
        for result in results:
            add(acc, result)
        return 0

    lax.fori_loop(0, slots // UNROLL, block, 0)
    keep_ref[...] = acc[:half]
    send_ref[...] = acc[half:2 * half].astype(BF16)
    for h in range(parts):
        row_sum_ref[h] = jnp.sum(packet_ref[:, parts + h].astype(F32), axis=0)


def half_kernel(keep_ref, recv_ref, out_ref):
    other = CORES - 1 - lax.axis_index(CORE)
    out_ref[...] = (keep_ref[...] + recv_ref[other].astype(F32)).astype(BF16)


def image_kernel(row_sum_ref, near_recv_ref, image_ref, *next_refs):
    parts, width = row_sum_ref.shape[0], row_sum_ref.shape[-1]
    for h in range(parts):
        value = (row_sum_ref[h] + jnp.sum(near_recv_ref[:, h].astype(F32), axis=0)).astype(image_ref.dtype)
        image_ref[:, h * width:(h + 1) * width] = value
        if next_refs:
            own_ref, copies_ref = next_refs
            own_ref[h] = value
            copies_ref[:, h] = jnp.broadcast_to(value[None], (copies_ref.shape[0],) + value.shape)


def call(kernel, name, in_specs, shapes, scratch, flops, moved, *args, vmem=12 * 1024):
    return pl.pallas_call(
        kernel,
        out_shape=tuple(jax.ShapeDtypeStruct(s, d) for s, d in shapes),
        in_specs=in_specs,
        out_specs=(VMEM,) * len(shapes),
        scratch_shapes=scratch,
        compiler_params=pltpu.CompilerParams(vmem_limit_bytes=vmem * 1024),
        cost_estimate=pl.CostEstimate(flops=flops, bytes_accessed=moved, transcendentals=0),
        name=name,
    )(*args)


def per_device(tile_values, tile_rows, tile_cols, tile_count, vectors):
    tiles = tile_values[0, 0]
    slots, tile = tiles.shape[0], tiles.shape[-1]
    vec_count, slice_len = vectors.shape
    parts = slice_len // tile
    peers, near = lax.axis_size(ROW), lax.axis_size(NEAR)
    piece = (parts, vec_count, tile)
    half = (near * parts, vec_count, tile)
    packets = (peers, 2 * parts, vec_count, tile)
    flops, moved = 2 * slots * vec_count * tile * tile, 2 * tiles.size
    acc = lambda n: [pltpu.VMEM((n + 1, vec_count, tile), F32)]

    def image(own, near_copies, dtype, again):
        near_recv = lax.all_to_all(near_copies, NEAR, 0, 0)
        row_seg = lax.all_gather(near_recv.reshape(half), CORE, axis=0, tiled=True)
        (packet,) = call(
            mirror_kernel, "mirror_products", [SMEM] + [VMEM] * 3,
            [(packets, BF16)], acc(peers * parts), flops, moved, places, tiles, row_seg, own)
        packet = lax.all_to_all(packet, ROW, 0, 0)
        keep, send, row_sum = call(
            direct_kernel, "direct_products", [SMEM] + [VMEM] * 2,
            [(half, F32), (half, BF16), (piece, F32)], acc(CORES * half[0]), flops, moved, places, tiles, packet)
        recv = lax.all_gather(send, CORE, axis=0)
        (chip,) = call(half_kernel, "chip_sum", [VMEM] * 2, [(half, BF16)], [], keep.size, 8 * keep.size, keep, recv)
        near_recv = lax.all_to_all(chip.reshape((near,) + piece), NEAR, 0, 0)
        shapes = [((vec_count, slice_len), dtype)]
        if again:
            shapes += [(piece, dtype), ((near,) + piece, dtype)]
        return call(image_kernel, "image", [VMEM] * 2, shapes, [], near_recv.size, 4 * near_recv.size, row_sum, near_recv)

    places = jnp.concatenate([tile_rows[0, 0], tile_cols[0, 0], tile_count[0]])
    places, tiles = call(
        load_kernel, "load", [ANY, VMEM], [(places.shape, jnp.int32), (tiles.shape, BF16)],
        [pltpu.SemaphoreType.DMA((TILE_COPIES,))], vectors.size, 2 * moved, tiles, places, vmem=50500)
    own, copies = call(
        start_kernel, "start", [VMEM], [(piece, BF16), ((near,) + piece, BF16)], [], vectors.size, 40 * vectors.size, vectors, vmem=57000)
    first_image, own, copies = image(own, copies, BF16, True)
    (second_image,) = image(own, copies, F32, False)
    return (first_image, second_image)


def solution(mesh):
    rows, cols = mesh.devices.shape
    split = Mesh(mesh.devices.reshape(rows, cols // CORES, CORES), (ROW, NEAR, CORE))
    col = (NEAR, CORE)
    whole = (ROW,) + col
    return jax.shard_map(
        per_device,
        mesh=split,
        in_specs=(P(ROW, col, None, None, None), P(ROW, col, None), P(ROW, col, None), P(ROW, col), P(None, whole)),
        out_specs=(P(None, whole), P(None, whole)),
        check_vma=False,
    )
```
